256 devices in a mesh: hist: 16 (over z, core), cand: 16 (over y, x).
Axes of the slice: x: 4, y: 4, z: 8, core: 2. Of those that a mesh axis runs over, the one named last changes fastest.
Arguments:
- history: bfloat16 [32, 256, 128, 512], P(None, 'hist', 'cand'), may hold values from -6 to 6
- candidates: bfloat16 [32, 2048, 512], P('hist', 'cand'), may hold values from -300 to 300
- selected: int32 [32, 16], replicated, may hold values from 0 to 255, as said below
- lengths: int32 [32], replicated, may hold values from 2048 to 32768
- kv_weight: bfloat16 [512, 1024], replicated, may hold values from -0.25 to 0.25
- query_weight: bfloat16 [512, 512], replicated, may hold values from -0.25 to 0.25
- out_weight: bfloat16 [512, 512], replicated, may hold values from -0.25 to 0.25
Outputs:
- interest: bfloat16 [32, 2048, 512], P('hist', 'cand')
The draws below stay inside these ranges and needn't reach their ends.
Inputs may be any that keep to these rules, and one draw needn't show every extreme that they name: `selected`: each user's ids are distinct; at most 2 of a user's ids lie in one range [h * 16, (h + 1) * 16), exactly 2 in some range for every user; every user has an id below 16.
All inputs are finite; a program needn't handle non-finite values.
Results may differ from the reference program's by a relative error of at most 0.007.
The reference program's roundings to bfloat16 on the way count: a program that leaves them out, or rounds other values in their place, can miss the bound.
Values may be sent and summed in bfloat16 or wider, within the bound.
A program may use at most 128 MiB of HBM per device.

```python
import jax
import jax.numpy as jnp
from jax import lax

D = 512
HEADS = 4
HD = 128
BLK = 128
NSEL = 16
LB = 16
U = 32
CAP = 2
SLOTS = 32
HIST_BLOCKS = 256
HIST_LEN = 32768
CANDS = 2048


def draw_selected(key, part):
    key = jax.random.fold_in(key, 11)
    first_key, second_key, third_key = jax.random.split(key, 3)
    owners = SLOTS // CAP
    items = jnp.arange(SLOTS, dtype=jnp.int32)
    item_owner = items // CAP
    noise = jax.random.randint(first_key, (U, SLOTS), 0, 1 << 20)
    hottest = jax.random.randint(second_key, (U, 1), 0, owners)
    scores = noise * SLOTS + items[None, :]
    scores = scores + jnp.where(item_owner[None, :] == hottest, 1 << 28, 0)
    scores = scores + jnp.where(items[None, :] == 0, 1 << 27, 0)
    chosen_values, picked = lax.top_k(scores, NSEL)
    picked = picked.astype(jnp.int32)
    perm_keys = jax.random.split(third_key, U * owners)
    orders = jax.vmap(lambda one_key: jax.random.permutation(one_key, LB))(perm_keys)
    orders = orders.reshape(U, owners * LB).astype(jnp.int32)
    pick_owner = picked // CAP
    pick_slot = picked % CAP
    local_block = jnp.take_along_axis(orders, pick_owner * LB + pick_slot, axis=1)
    return (pick_owner * LB + local_block).astype(jnp.int32)


def draw_lengths(key, part):
    key = jax.random.fold_in(key, 12)
    first_key, second_key = jax.random.split(key)
    drawn = jax.random.randint(first_key, (U,), LB * BLK, HIST_LEN + 1)
    longest = jax.random.randint(second_key, (), 0, U)
    return jnp.where(jnp.arange(U, dtype=jnp.int32) == longest, HIST_LEN, drawn).astype(jnp.int32)


def draw_candidates(key, part):
    key = jax.random.fold_in(key, 13)
    first_key = jax.random.fold_in(key, 0)
    values = jnp.clip(jax.random.normal(first_key, (U, CANDS, D), jnp.float32), -5.0, 5.0)
    return values.astype(jnp.bfloat16)


def steps_of(key, dims, cuts, least, high):
    level = 1.0
    for position, blocks in cuts:
        heights = jax.random.uniform(jax.random.fold_in(jax.random.fold_in(key, 6), position), (blocks,), jnp.float32, least / len(cuts), high / len(cuts))
        level = level * jnp.repeat(jnp.exp(heights), dims[position] // blocks).reshape((-1,) + (1,) * (len(dims) - 1 - position))
    return level


def centred(own_key, shape, spread, reach, pieces=(), held_as=jnp.bfloat16):
    values = spread * jax.random.normal(own_key, shape, jnp.float32)
    if pieces:
        values = values * steps_of(own_key, shape, pieces, -0.22, 0.18)
    return jnp.clip(values, -reach, reach).astype(held_as)


def setup_inputs(seed: int = 0) -> dict:
    seeds = jax.random.split(jax.random.key(seed), 8)
    history = centred(seeds[0], (U, HIST_BLOCKS, BLK, D), 1.0, 6.0, ((1, 16), (2, 16)))
    candidates = draw_candidates(jax.random.fold_in(seeds[7], 71), 0)
    selected = draw_selected(jax.random.fold_in(seeds[7], 71), 0)
    lengths = draw_lengths(jax.random.fold_in(seeds[7], 71), 0)
    kv_weight = centred(seeds[4], (D, 2 * D), D ** -0.5, 0.25)
    query_weight = centred(seeds[5], (D, D), D ** -0.5, 0.25)
    out_weight = centred(seeds[6], (D, D), D ** -0.5, 0.25)
    return {"history": history, "candidates": candidates, "selected": selected, "lengths": lengths, "kv_weight": kv_weight, "query_weight": query_weight, "out_weight": out_weight}


def reference(history, candidates, selected, lengths, kv_weight, query_weight, out_weight):
    def one_user(operands):
        user_hist, user_cands, user_sel, user_len = operands
        blocks = user_hist.reshape(HIST_BLOCKS, BLK, D)[user_sel]
        rows = blocks.reshape(NSEL * BLK, D)
        kv_rows = jnp.dot(rows, kv_weight, preferred_element_type=jnp.float32).astype(jnp.bfloat16)
        positions = (user_sel[:, None] * BLK + jnp.arange(BLK, dtype=jnp.int32)[None, :]).reshape(-1)
        valid = positions < user_len
        queries = jnp.dot(user_cands, query_weight, preferred_element_type=jnp.float32).astype(jnp.bfloat16)
        q_heads = queries.reshape(CANDS, HEADS, HD).astype(jnp.float32)
        k_heads = kv_rows[:, :D].reshape(NSEL * BLK, HEADS, HD).astype(jnp.float32)
        v_heads = kv_rows[:, D:].reshape(NSEL * BLK, HEADS, HD).astype(jnp.float32)
        scores = jnp.einsum("chd,khd->hck", q_heads, k_heads) * (HD ** -0.5)
        scores = jnp.where(valid[None, None, :], scores, jnp.float32(-1e30))
        largest = jnp.max(scores, axis=-1, keepdims=True)
        expo = jnp.exp(scores - largest)
        weights = (expo / jnp.sum(expo, axis=-1, keepdims=True)).astype(jnp.bfloat16)
        weights = lax.optimization_barrier(weights).astype(jnp.float32)
        mixed = jnp.einsum("hck,khd->chd", weights, v_heads).reshape(CANDS, D).astype(jnp.bfloat16)
        return jnp.dot(mixed, out_weight, preferred_element_type=jnp.float32).astype(jnp.bfloat16)

    return lax.map(one_user, (history, candidates, selected, lengths))
```

```python
import functools

import jax
import jax.numpy as jnp
from jax import lax
from jax.experimental import pallas as pl
from jax.experimental.pallas import tpu as pltpu
from jax.sharding import PartitionSpec as P

MESH = pl.DeviceIdType.MESH
HEADS = 4
HD = 128
BLK = 128
NSEL = 16
D = 512
U = 32
LB = 16
OWN = 16
ROWS = 8
C = 128
SCALE = HD ** -0.5 * 1.4426950408889634
NT = (((1,), (1,)), ((), ()))


def kernel(sel_ref, len_ref, hist_hbm, cand_hbm, kvw_hbm, qw_hbm, ow_hbm, out_ref,
           hist_v, pick, zbuf0, zbuf1, cand_v, kvw, qw, ow, gat, qall, k_v, v_v, osend, ostat, orecv, rstat, ids,
           in_sem, zs_sem, zr_sem, xs_sem, xr_sem, qs_sem, qr_sem, os_sem, or_sem, ss_sem, sr_sem):
    zbuf = (zbuf0, zbuf1)
    h = lax.axis_index("hist")
    c = lax.axis_index("cand")
    z, core = h // 2, h % 2
    y, x = c // 4, c % 4

    hist_parts = 4
    per = U // hist_parts
    hist_copies = [
        pltpu.make_async_copy(hist_hbm.at[pl.ds(p * per, per)], hist_v.at[pl.ds(p * per, per)], in_sem.at[p])
        for p in range(hist_parts)
    ]
    for cp in hist_copies:
        cp.start()
    small = [
        pltpu.make_async_copy(cand_hbm, cand_v, in_sem.at[4]),
        pltpu.make_async_copy(qw_hbm, qw, in_sem.at[5]),
        pltpu.make_async_copy(kvw_hbm, kvw, in_sem.at[6]),
        pltpu.make_async_copy(ow_hbm, ow, in_sem.at[7]),
    ]
    for cp in small:
        cp.start()

    zpeers = []
    for dz in (4, 3, 5, 2, 6, 1, 7, 0):
        for dc in (0, 1):
            if dz == 0 and dc == 0:
                continue
            zpeers.append(lax.rem(z + dz, 8) * 2 + lax.rem(core + dc, 2))
    xpeers = [lax.rem(x + d, 4) for d in (2, 1, 3)]
    ypeers = [lax.rem(y + d, 4) for d in (2, 1, 3)]

    barrier = pltpu.get_barrier_semaphore()
    for hp in zpeers:
        pl.semaphore_signal(barrier, inc=1, device_id=(hp, c), device_id_type=MESH)
    for xp in xpeers:
        pl.semaphore_signal(barrier, inc=1, device_id=(h, y * 4 + xp), device_id_type=MESH)
    for yp in ypeers:
        pl.semaphore_signal(barrier, inc=1, device_id=(h, yp * 4 + x), device_id_type=MESH)

    def find(u, carry):
        first = jnp.int32(0)
        second = jnp.int32(0)
        for n in range(NSEL):
            one = sel_ref[u, n]
            mine = lax.shift_right_logical(one, 4) == h
            second = jnp.where(mine, first, second)
            first = jnp.where(mine, one & 15, first)
        ids[u, 0] = first
        ids[u, 1] = second
        return carry

    lax.fori_loop(0, U, find, 0)

    for cp in hist_copies:
        cp.wait()

    def choose(u, carry):
        top = hist_v[u, ids[u, 0]]
        low = hist_v[u, ids[u, 1]]
        pick[u] = jnp.concatenate([top, low], axis=0)
        return carry

    lax.fori_loop(0, U, choose, 0)

    pl.semaphore_wait(barrier, 21)

    for t in range(2):
        for hp in zpeers:
            pltpu.make_async_remote_copy(
                src_ref=pick.at[2 * hp + t], dst_ref=zbuf[t].at[h], send_sem=zs_sem.at[t], recv_sem=zr_sem.at[t],
                device_id=(hp, c), device_id_type=MESH,
            ).start()
        zbuf[t][h] = pick[2 * h + t]

    small[0].wait()
    small[1].wait()
    q_copies = []
    for t in range(2):
        qall[t, y] = jnp.dot(cand_v[t], qw[...], preferred_element_type=jnp.float32).astype(jnp.bfloat16)
        for i, yp in enumerate(ypeers):
            cp = pltpu.make_async_remote_copy(
                src_ref=qall.at[t, y], dst_ref=qall.at[t, y], send_sem=qs_sem.at[t, i], recv_sem=qr_sem.at[t, i],
                device_id=(h, yp * 4 + x), device_id_type=MESH,
            )
            cp.start()
            q_copies.append(cp)
    small[2].wait()
    small[3].wait()

    v_v[...] = jnp.ones_like(v_v)
    lane = lax.broadcasted_iota(jnp.int32, (1, 4 * C), 1)
    lane_n = lax.shift_right_logical(lane, 3) & 15
    lane_row = (y * 4 + lax.shift_right_logical(lane, 7)) * ROWS + (lane & 7)
    col = lax.broadcasted_iota(jnp.int32, (C, C), 1)

    all_copies = list(q_copies)
    for t in range(2):
        user = 2 * h + t
        sel = [sel_ref[user, n] for n in range(NSEL)]
        own = [lax.shift_right_logical(s, 4) for s in sel]
        slot = []
        for n in range(NSEL):
            later = jnp.int32(0)
            for m in range(n + 1, NSEL):
                later = later | (own[m] == own[n]).astype(jnp.int32)
            slot.append(later)
        idv = jnp.zeros((1, 4 * C), jnp.int32)
        for n in range(NSEL):
            idv = jnp.where(lane_n == n, sel[n], idv)
        bias = jnp.where(idv * BLK + lane_row < len_ref[user], 0.0, -1e30).astype(jnp.float32)

        pltpu.make_async_copy(zbuf[t].at[pl.ds(0, 15)], zbuf[t].at[pl.ds(0, 15)], zr_sem.at[t]).wait()
        for n in range(0, NSEL, 2):
            pair = []
            for m in (n, n + 1):
                both = zbuf[t][own[m]]
                pair.append(jnp.where(slot[m] == 0, both[:ROWS], both[ROWS:]))
            gat[t, x, n * ROWS:(n + 2) * ROWS] = jnp.concatenate(pair, axis=0)
        x_copies = []
        for i, xp in enumerate(xpeers):
            cp = pltpu.make_async_remote_copy(
                src_ref=gat.at[t, x], dst_ref=gat.at[t, x], send_sem=xs_sem.at[t, i], recv_sem=xr_sem.at[t, i],
                device_id=(h, y * 4 + xp), device_id_type=MESH,
            )
            cp.start()
            x_copies.append(cp)
        for cp in x_copies:
            cp.wait_recv()
        rows = gat[t].reshape(4 * C, D)
        k_v[...] = jnp.dot(rows, kvw[:, :D], preferred_element_type=jnp.float32).astype(jnp.bfloat16)
        values = jnp.dot(rows, kvw[:, D:], preferred_element_type=jnp.float32).astype(jnp.bfloat16)
        for hd in range(HEADS):
            v_v[:, hd * 256:hd * 256 + HD] = values[:, hd * HD:(hd + 1) * HD]
        for cp in q_copies[3 * t:3 * t + 3]:
            cp.wait_recv()

        def attend(yp):
            stat = jnp.zeros((C, C), jnp.float32)
            parts = []
            for hd in range(HEADS):
                s = lax.dot_general(
                    qall[t, yp, :, hd * HD:(hd + 1) * HD], k_v[:, hd * HD:(hd + 1) * HD], NT,
                    preferred_element_type=jnp.float32,
                ) * SCALE + bias
                m = jnp.max(s, axis=1, keepdims=True)
                p = jnp.exp2(s - m).astype(jnp.bfloat16)
                o = jnp.dot(p, v_v[:, hd * 256:(hd + 1) * 256], preferred_element_type=jnp.float32)
                l = o[:, HD:]
                parts.append((o[:, :HD] / l).astype(jnp.bfloat16))
                stat = jnp.where(col == hd, m, stat)
                stat = jnp.where(col == HEADS + hd, l, stat)
            return jnp.concatenate(parts, axis=1), stat.T[:8]

        for i, yp in enumerate(ypeers):
            part, stat = attend(yp)
            osend[t, i] = part
            ostat[t, i] = stat
            for src, dst, ssem, rsem in ((osend, orecv, os_sem, or_sem), (ostat, rstat, ss_sem, sr_sem)):
                cp = pltpu.make_async_remote_copy(
                    src_ref=src.at[t, i], dst_ref=dst.at[t, i], send_sem=ssem.at[t, i], recv_sem=rsem.at[t, i],
                    device_id=(h, yp * 4 + x), device_id_type=MESH,
                )
                cp.start()
                all_copies.append(cp)
        part, stat = attend(y)
        orecv[t, 3] = part
        rstat[t, 3] = stat
        for cp in x_copies:
            cp.wait_send()

    for cp in q_copies:
        cp.wait_send()
    out_copies = all_copies[6:]
    for t in range(2):
        for cp in out_copies[6 * t:6 * t + 6]:
            cp.wait_recv()
        stats = [rstat[t, k] for k in range(4)]
        top = jnp.maximum(jnp.maximum(stats[0][:4], stats[1][:4]), jnp.maximum(stats[2][:4], stats[3][:4]))
        parts = [s[4:] * jnp.exp2(s[:4] - top) for s in stats]
        total = (parts[0] + parts[1]) + (parts[2] + parts[3])
        wts = jnp.concatenate([p / total for p in parts] + [jnp.zeros((C - 16, C), jnp.float32)], axis=0).T
        mixed = []
        for hd in range(HEADS):
            acc = jnp.zeros((C, HD), jnp.float32)
            for k in range(4):
                acc = acc + wts[:, 4 * k + hd:4 * k + hd + 1] * orecv[t, k, :, hd * HD:(hd + 1) * HD].astype(jnp.float32)
            mixed.append(acc.astype(jnp.bfloat16))
        mixed = jnp.concatenate(mixed, axis=1)
        out_ref[t] = jnp.dot(mixed, ow[...], preferred_element_type=jnp.float32).astype(jnp.bfloat16)
    for cp in out_copies:
        cp.wait_send()
    for t in range(2):
        pltpu.make_async_copy(zbuf[t].at[pl.ds(0, 15)], zbuf[t].at[pl.ds(0, 15)], zs_sem.at[t]).wait()


def per_device(history, candidates, selected, lengths, kv_weight, query_weight, out_weight):
    smem = pl.BlockSpec(memory_space=pltpu.SMEM)
    any_ = pl.BlockSpec(memory_space=pl.ANY)
    bf = jnp.bfloat16
    dma = pltpu.SemaphoreType.DMA
    return pl.pallas_call(
        kernel,
        out_shape=jax.ShapeDtypeStruct((2, C, D), bf),
        in_specs=[smem, smem, any_, any_, any_, any_, any_],
        out_specs=pl.BlockSpec(memory_space=pltpu.VMEM),
        scratch_shapes=[
            pltpu.VMEM((U, LB, ROWS, D), bf),
            pltpu.VMEM((U, 2 * ROWS, D), bf),
            pltpu.VMEM((OWN, 2 * ROWS, D), bf),
            pltpu.VMEM((OWN, 2 * ROWS, D), bf),
            pltpu.VMEM((2, C, D), bf),
            pltpu.VMEM((D, 2 * D), bf),
            pltpu.VMEM((D, D), bf),
            pltpu.VMEM((D, D), bf),
            pltpu.VMEM((2, 4, C, D), bf),
            pltpu.VMEM((2, 4, C, D), bf),
            pltpu.VMEM((4 * C, D), bf),
            pltpu.VMEM((4 * C, HEADS * 256), bf),
            pltpu.VMEM((2, 3, C, D), bf),
            pltpu.VMEM((2, 3, 8, C), jnp.float32),
            pltpu.VMEM((2, 4, C, D), bf),
            pltpu.VMEM((2, 4, 8, C), jnp.float32),
            pltpu.SMEM((U, 2), jnp.int32),
            dma((8,)),
            dma((2,)), dma((2,)),
            dma((2, 3)), dma((2, 3)),
            dma((2, 3)), dma((2, 3)),
            dma((2, 3)), dma((2, 3)),
            dma((2, 3)), dma((2, 3)),
        ],
        compiler_params=pltpu.CompilerParams(
            collective_id=0, has_side_effects=True, vmem_limit_bytes=48 * 1024 * 1024
        ),
    )(selected, lengths, history, candidates, kv_weight, query_weight, out_weight)


def solution(mesh):
    return jax.shard_map(
        per_device,
        mesh=mesh,
        in_specs=(P(None, "hist", "cand", None), P("hist", "cand", None), P(), P(), P(), P(), P()),
        out_specs=P("hist", "cand", None),
        check_vma=False,
    )
```

```python
import jax
import jax.numpy as jnp
from jax import lax
from jax.experimental import pallas as pl
from jax.experimental.pallas import tpu as pltpu
from jax.sharding import PartitionSpec as P

MESH = pl.DeviceIdType.MESH
HEADS = 4
HD = 128
BLK = 128
NSEL = 16
D = 512
U = 32
LB = 16
OWN_RANGES = 16
ROWS = 8
C = 128
HALF = C // 2
SCALE = HD ** -0.5 * 1.4426950408889634
NT = (((1,), (1,)), ((), ()))
OPP, LEFT, RIGHT, OWN = 0, 1, 2, 3


def spread(buf, peers, send_sem, recv_sem):
    copies = [
        pltpu.make_async_remote_copy(
            src_ref=buf.at[OWN], dst_ref=buf.at[s], send_sem=send_sem.at[s], recv_sem=recv_sem.at[s],
            device_id=peers[s], device_id_type=MESH,
        )
        for s in (OPP, LEFT, RIGHT)
    ]

    def start():
        for cp in copies:
            cp.start()

    def arrived(*slots):
        for s in slots:
            copies[s].wait_recv()

    def sent():
        for cp in copies:
            cp.wait_send()

    return start, arrived, sent


def kernel(sel_ref, len_ref, hist_hbm, cand_hbm, kvw_hbm, qw_hbm, ow_hbm, out_ref,
           hist0, hist1, hist2, hist3, pick, zbuf0, zbuf1, cand_v, kvw, qw, ow, gat, qall, k_v, v_v,
           osend, ostat, orecv, rstat,
           in_sem, zs_sem, zr_sem, nb_sem, xs_sem, xr_sem, qs_sem, qr_sem, os_sem, or_sem, ss_sem, sr_sem):
    hist_v = (hist0, hist1, hist2, hist3)
    zbuf = (zbuf0, zbuf1)
    h = lax.axis_index("hist")
    c = lax.axis_index("cand")
    z, core = h // 2, h % 2
    y, x = c // 4, c % 4
    sibling = (2 * z + 1 - core, c)

    kpos = jnp.where(core == 0, x, y)
    cpos = jnp.where(core == 0, y, x)
    kstep = jnp.where(core == 0, 1, 4)
    cstep = 5 - kstep

    def kdev(d):
        return (h, cpos * cstep + ((kpos + d) & 3) * kstep)

    def cdev(d):
        return (h, ((cpos + d) & 3) * cstep + kpos * kstep)

    kpeers = {OPP: kdev(2), LEFT: kdev(1), RIGHT: kdev(3)}
    cpeers = {OPP: cdev(2), LEFT: cdev(1), RIGHT: cdev(3)}

    hist_copies = [
        pltpu.make_async_copy(hist_hbm.at[:, 2 * (p % 2) + p // 2], hist_v[p], in_sem.at[p]) for p in range(4)
    ]
    small = [
        pltpu.make_async_copy(cand_hbm, cand_v, in_sem.at[4]),
        pltpu.make_async_copy(qw_hbm, qw, in_sem.at[5]),
        pltpu.make_async_copy(kvw_hbm, kvw, in_sem.at[6]),
        pltpu.make_async_copy(ow_hbm, ow, in_sem.at[7]),
    ]
    for cp in hist_copies + small:
        cp.start()

    zorder = (4, 3, 5, 2, 6, 1, 7)
    zpeers = [lax.rem(z + dz, 8) for dz in zorder]

    barrier = pltpu.get_barrier_semaphore()
    for zp in zpeers:
        for k in range(2):
            pl.semaphore_signal(barrier, inc=1, device_id=(2 * zp + k, c), device_id_type=MESH)
    for dev in [sibling] + [f(d) for f in (kdev, cdev) for d in (2, 1, 3)]:
        pl.semaphore_signal(barrier, inc=1, device_id=dev, device_id_type=MESH)

    def choose(p):
        hist_copies[p].wait()

        def one_user(zp, carry):
            u = 4 * zp + 2 * (p % 2) + p // 2
            first = jnp.int32(0)
            second = jnp.int32(0)
            for n in range(NSEL):
                one = sel_ref[n, u]
                mine = lax.shift_right_logical(one, 4) == h
                second = jnp.where(mine, first, second)
                first = jnp.where(mine, one & 15, first)
            pick[p, zp] = jnp.concatenate([hist_v[p][zp, first], hist_v[p][zp, second]], axis=0)
            return carry

        lax.fori_loop(0, 8, one_user, 0)

    def zsend(p):
        for zp in zpeers:
            pltpu.make_async_remote_copy(
                src_ref=pick.at[p, zp], dst_ref=zbuf[p // 2].at[h], send_sem=zs_sem.at[p], recv_sem=zr_sem.at[p // 2],
                device_id=(2 * zp + p % 2, c), device_id_type=MESH,
            ).start()

    def zsent(p):
        pltpu.make_async_copy(zbuf0.at[pl.ds(0, 7)], zbuf0.at[pl.ds(0, 7)], zs_sem.at[p]).wait()

    nb_copies = [
        pltpu.make_async_remote_copy(
            src_ref=pick.at[2 * t + 1 - core, z], dst_ref=zbuf[t].at[h], send_sem=nb_sem.at[t], recv_sem=zr_sem.at[t],
            device_id=sibling, device_id_type=MESH,
        )
        for t in range(2)
    ]

    choose(0)
    pl.semaphore_wait(barrier, 21)
    zsend(0)
    choose(1)
    zsend(1)
    nb_copies[0].start()
    zbuf0[h] = pick[core, z]

    small[0].wait()
    small[1].wait()
    rows_to = [spread(gat.at[t], kpeers, xs_sem.at[t], xr_sem.at[t]) for t in range(2)]
    queries_to = [spread(qall.at[t], cpeers, qs_sem.at[t], qr_sem.at[t]) for t in range(2)]
    for t in range(2):
        qall[t, OWN] = jnp.dot(cand_v[t], qw[...], preferred_element_type=jnp.float32).astype(jnp.bfloat16)
        queries_to[t][0]()

    choose(2)
    choose(3)
    nb_copies[1].start()
    zbuf1[h] = pick[2 + core, z]

    zsent(0)
    zsend(2)

    v_v[...] = jnp.ones_like(v_v)
    lane = lax.broadcasted_iota(jnp.int32, (1, 4 * C), 1)
    lane_slot = lax.shift_right_logical(lane, 7)
    lane_n = lax.shift_right_logical(lane, 3) & 15
    lane_k = jnp.where(lane_slot == OPP, 2, jnp.where(lane_slot == LEFT, 3, jnp.where(lane_slot == RIGHT, 1, 0)))
    lane_row = (cpos * cstep + ((kpos + lane_k) & 3) * kstep) * ROWS + (lane & 7)
    col = lax.broadcasted_iota(jnp.int32, (2 * C, C), 1)

    def mask(t):
        user = 2 * h + t
        idv = jnp.zeros((1, 4 * C), jnp.int32)
        for n in range(NSEL):
            idv = jnp.where(lane_n == n, sel_ref[n, user], idv)
        return jnp.where(idv * BLK + lane_row < len_ref[user], 0.0, -1e30).astype(jnp.float32)

    def compact(t):
        user = 2 * h + t
        own = [lax.shift_right_logical(sel_ref[n, user], 4) for n in range(NSEL)]
        pltpu.make_async_copy(zbuf[t].at[pl.ds(0, 15)], zbuf[t].at[pl.ds(0, 15)], zr_sem.at[t]).wait()
        for n in range(0, NSEL, 2):
            pair = []
            for m in (n, n + 1):
                later = jnp.int32(0)
                for o in range(m + 1, NSEL):
                    later = later | (own[o] == own[m]).astype(jnp.int32)
                both = zbuf[t][own[m]]
                pair.append(jnp.where(later == 0, both[:ROWS], both[ROWS:]))
            gat[t, OWN, n * ROWS:(n + 2) * ROWS] = jnp.concatenate(pair, axis=0)

    def project(t, slots):
        for s in slots:
            kv = jnp.dot(gat[t, s], kvw[...], preferred_element_type=jnp.float32).astype(jnp.bfloat16)
            k_v[s * C:(s + 1) * C] = kv[:, :D]
            for hd in range(HEADS):
                v_v[s * C:(s + 1) * C, hd * 256:hd * 256 + HD] = kv[:, D + hd * HD:D + (hd + 1) * HD]

    out_copies = {}

    def send_out(t, s):
        to = cdev({OPP: 2, LEFT: 3, RIGHT: 1}[s])
        for kind, (src, dst, ssem, rsem) in enumerate(
            ((osend, orecv, os_sem, or_sem), (ostat, rstat, ss_sem, sr_sem))
        ):
            cp = pltpu.make_async_remote_copy(
                src_ref=src.at[t, s], dst_ref=dst.at[t, s], send_sem=ssem.at[t, s], recv_sem=rsem.at[t, s],
                device_id=to, device_id_type=MESH,
            )
            cp.start()
            out_copies[t, s, kind] = cp

    def attend(t, bias, pair):
        stat = jnp.zeros((2 * C, C), jnp.float32)
        parts = []
        for hd in range(HEADS):
            q = qall[t, pair:pair + 2, :, hd * HD:(hd + 1) * HD].reshape(2 * C, HD)
            s = lax.dot_general(q, k_v[:, hd * HD:(hd + 1) * HD], NT, preferred_element_type=jnp.float32) * SCALE + bias
            m = jnp.max(s, axis=1, keepdims=True)
            p = jnp.exp2(s - m).astype(jnp.bfloat16)
            o = jnp.dot(p, v_v[:, hd * 256:(hd + 1) * 256], preferred_element_type=jnp.float32)
            l = o[:, HD:]
            parts.append((o[:, :HD] / l).astype(jnp.bfloat16))
            stat = jnp.where(col == hd, m, stat)
            stat = jnp.where(col == HEADS + hd, l, stat)
        part = jnp.concatenate(parts, axis=1)
        stat = stat.T[:8]
        for i in range(2):
            s = pair + i
            if s == OWN:
                orecv[t, OWN] = part[i * C:(i + 1) * C]
                rstat[t, OWN] = stat[:, i * C:(i + 1) * C]
            else:
                osend[t, s] = part[i * C:(i + 1) * C]
                ostat[t, s] = stat[:, i * C:(i + 1) * C]
                send_out(t, s)

    def finish(t):
        for s in (OPP, LEFT, RIGHT):
            for kind in range(2):
                out_copies[t, s, kind].wait_recv()
        stats = [rstat[t, k] for k in range(4)]
        top = jnp.maximum(jnp.maximum(stats[0][:4], stats[1][:4]), jnp.maximum(stats[2][:4], stats[3][:4]))
        parts = [s[4:] * jnp.exp2(s[:4] - top) for s in stats]
        total = (parts[0] + parts[1]) + (parts[2] + parts[3])
        wts = jnp.concatenate([p / total for p in parts] + [jnp.zeros((C - 16, C), jnp.float32)], axis=0).T
        mixed = []
        for hd in range(HEADS):
            acc = jnp.zeros((C, HD), jnp.float32)
            for k in range(4):
                acc = acc + wts[:, 4 * k + hd:4 * k + hd + 1] * orecv[t, k, :, hd * HD:(hd + 1) * HD].astype(jnp.float32)
            mixed.append(acc.astype(jnp.bfloat16))
        mixed = jnp.concatenate(mixed, axis=1)
        out_ref[t] = jnp.dot(mixed, ow[...], preferred_element_type=jnp.float32).astype(jnp.bfloat16)

    bias0, bias1 = mask(0), mask(1)
    compact(0)
    rows_to[0][0]()
    zsent(1)
    zsend(3)
    small[2].wait()
    project(0, (OWN,))
    rows_to[0][1](LEFT, RIGHT)
    project(0, (LEFT, RIGHT))
    rows_to[0][1](OPP)
    project(0, (OPP,))
    queries_to[0][1](OPP, LEFT, RIGHT)
    attend(0, bias0, 0)
    compact(1)
    rows_to[1][0]()
    attend(0, bias0, 2)
    project(1, (OWN,))
    small[3].wait()
    finish(0)
    rows_to[1][1](LEFT, RIGHT)
    project(1, (LEFT, RIGHT))
    rows_to[1][1](OPP)
    project(1, (OPP,))
    queries_to[1][1](OPP, LEFT, RIGHT)
    attend(1, bias1, 0)
    attend(1, bias1, 2)
    finish(1)

    for t in range(2):
        rows_to[t][2]()
        queries_to[t][2]()
        zsent(2 + t)
        nb_copies[t].wait_send()
    for cp in out_copies.values():
        cp.wait_send()


def per_device(history, candidates, selected, lengths, kv_weight, query_weight, out_weight):
    smem = pl.BlockSpec(memory_space=pltpu.SMEM)
    any_ = pl.BlockSpec(memory_space=pl.ANY)
    bf = jnp.bfloat16
    dma = pltpu.SemaphoreType.DMA
    return pl.pallas_call(
        kernel,
        out_shape=jax.ShapeDtypeStruct((2, C, D), bf),
        in_specs=[smem, smem, any_, any_, any_, any_, any_],
        out_specs=pl.BlockSpec(memory_space=pltpu.VMEM),
        scratch_shapes=[pltpu.VMEM((8, LB, ROWS, D), bf)] * 4
        + [pltpu.VMEM((4, 8, 2 * ROWS, D), bf)]
        + [pltpu.VMEM((OWN_RANGES, 2 * ROWS, D), bf)] * 2
        + [
            pltpu.VMEM((2, C, D), bf),
            pltpu.VMEM((D, 2 * D), bf),
            pltpu.VMEM((D, D), bf),
            pltpu.VMEM((D, D), bf),
            pltpu.VMEM((2, 4, C, D), bf),
            pltpu.VMEM((2, 4, C, D), bf),
            pltpu.VMEM((4 * C, D), bf),
            pltpu.VMEM((4 * C, HEADS * 256), bf),
            pltpu.VMEM((2, 3, C, D), bf),
            pltpu.VMEM((2, 3, 8, C), jnp.float32),
            pltpu.VMEM((2, 4, C, D), bf),
            pltpu.VMEM((2, 4, 8, C), jnp.float32),
            dma((8,)),
            dma((4,)), dma((2,)), dma((2,)),
            dma((2, 3)), dma((2, 3)),
            dma((2, 3)), dma((2, 3)),
            dma((2, 3)), dma((2, 3)),
            dma((2, 3)), dma((2, 3)),
        ],
        compiler_params=pltpu.CompilerParams(
            collective_id=0, has_side_effects=True, vmem_limit_bytes=60 * 1024 * 1024
        ),
    )(selected.T, lengths, history.reshape(8, 4, LB, ROWS, D), candidates, kv_weight, query_weight, out_weight)


def solution(mesh):
    return jax.shard_map(
        per_device,
        mesh=mesh,
        in_specs=(P(None, "hist", "cand", None), P("hist", "cand", None), P(), P(), P(), P(), P()),
        out_specs=P("hist", "cand", None),
        check_vma=False,
    )
```

```python
import jax
import jax.numpy as jnp
from jax import lax
from jax.experimental import pallas as pl
from jax.experimental.pallas import tpu as pltpu
from jax.sharding import PartitionSpec as P

MESH = pl.DeviceIdType.MESH
HEADS = 4
HD = 128
BLK = 128
NSEL = 16
D = 512
U = 32
LB = 16
OWN_RANGES = 16
ROWS = 8
C = 128
HALF = C // 2
SCALE = HD ** -0.5 * 1.4426950408889634
NT = (((1,), (1,)), ((), ()))
OPP, LEFT, RIGHT, OWN = 0, 1, 2, 3


def spread(buf, peers, send_sem, recv_sem):
    copies = [
        pltpu.make_async_remote_copy(
            src_ref=buf.at[OWN], dst_ref=buf.at[s], send_sem=send_sem.at[s], recv_sem=recv_sem.at[s],
            device_id=peers[s], device_id_type=MESH,
        )
        for s in (OPP, LEFT, RIGHT)
    ]

    def start():
        for cp in copies:
            cp.start()

    def arrived(*slots):
        for s in slots:
            copies[s].wait_recv()

    def sent():
        for cp in copies:
            cp.wait_send()

    return start, arrived, sent


def kernel(sel_ref, len_ref, hist_hbm, cand_hbm, kvw_hbm, qw_hbm, ow_hbm, out_ref,
           hist0, hist1, hist2, hist3, pick, zbuf0, zbuf1, cand_v, kvw, qw, ow, gat, qall, k_v, v_v,
           osend, ostat, orecv, rstat,
           in_sem, zs_sem, zr_sem, nb_sem, xs_sem, xr_sem, qs_sem, qr_sem, os_sem, or_sem, ss_sem, sr_sem):
    hist_v = (hist0, hist1, hist2, hist3)
    zbuf = (zbuf0, zbuf1)
    h = lax.axis_index("hist")
    c = lax.axis_index("cand")
    z, core = h // 2, h % 2
    y, x = c // 4, c % 4
    sibling = (2 * z + 1 - core, c)

    kpos = jnp.where(core == 0, x, y)
    cpos = jnp.where(core == 0, y, x)
    kstep = jnp.where(core == 0, 1, 4)
    cstep = 5 - kstep

    def kdev(d):
        return (h, cpos * cstep + ((kpos + d) & 3) * kstep)

    def cdev(d):
        return (h, ((cpos + d) & 3) * cstep + kpos * kstep)

    kpeers = {OPP: kdev(2), LEFT: kdev(1), RIGHT: kdev(3)}
    cpeers = {OPP: cdev(2), LEFT: cdev(1), RIGHT: cdev(3)}

    hist_copies = [
        pltpu.make_async_copy(hist_hbm.at[:, 2 * (p % 2) + p // 2], hist_v[p], in_sem.at[p]) for p in range(4)
    ]
    small = [
        pltpu.make_async_copy(cand_hbm, cand_v, in_sem.at[4]),
        pltpu.make_async_copy(qw_hbm, qw, in_sem.at[5]),
        pltpu.make_async_copy(kvw_hbm, kvw, in_sem.at[6]),
        pltpu.make_async_copy(ow_hbm, ow, in_sem.at[7]),
    ]
    for cp in hist_copies + small:
        cp.start()

    zorder = (4, 3, 5, 2, 6, 1, 7)
    zpeers = [lax.rem(z + dz, 8) for dz in zorder]

    barrier = pltpu.get_barrier_semaphore()
    for zp in zpeers:
        for k in range(2):
            pl.semaphore_signal(barrier, inc=1, device_id=(2 * zp + k, c), device_id_type=MESH)
    for dev in [sibling] + [f(d) for f in (kdev, cdev) for d in (2, 1, 3)]:
        pl.semaphore_signal(barrier, inc=1, device_id=dev, device_id_type=MESH)

    def choose(p):
        hist_copies[p].wait()

        def one_user(zp, carry):
            u = 4 * zp + 2 * (p % 2) + p // 2
            first = jnp.int32(0)
            second = jnp.int32(0)
            for n in range(NSEL):
                one = sel_ref[n, u]
                mine = lax.shift_right_logical(one, 4) == h
                second = jnp.where(mine, first, second)
                first = jnp.where(mine, one & 15, first)
            pick[p, zp] = jnp.concatenate([hist_v[p][zp, first], hist_v[p][zp, second]], axis=0)
            return carry

        lax.fori_loop(0, 8, one_user, 0)

    def zsend(p):
        for zp in zpeers:
            pltpu.make_async_remote_copy(
                src_ref=pick.at[p, zp], dst_ref=zbuf[p // 2].at[h], send_sem=zs_sem.at[p], recv_sem=zr_sem.at[p // 2],
                device_id=(2 * zp + p % 2, c), device_id_type=MESH,
            ).start()

    def zsent(p):
        pltpu.make_async_copy(zbuf0.at[pl.ds(0, 7)], zbuf0.at[pl.ds(0, 7)], zs_sem.at[p]).wait()

    nb_copies = [
        pltpu.make_async_remote_copy(
            src_ref=pick.at[2 * t + 1 - core, z], dst_ref=zbuf[t].at[h], send_sem=nb_sem.at[t], recv_sem=zr_sem.at[t],
            device_id=sibling, device_id_type=MESH,
        )
        for t in range(2)
    ]

    choose(0)
    pl.semaphore_wait(barrier, 21)
    zsend(0)
    choose(1)
    zsend(1)
    nb_copies[0].start()
    zbuf0[h] = pick[core, z]

    small[0].wait()
    small[1].wait()
    rows_to = [spread(gat.at[t], kpeers, xs_sem.at[t], xr_sem.at[t]) for t in range(2)]
    queries_to = [spread(qall.at[t], cpeers, qs_sem.at[t], qr_sem.at[t]) for t in range(2)]
    for t in range(2):
        qall[t, OWN] = jnp.dot(cand_v[t], qw[...], preferred_element_type=jnp.float32).astype(jnp.bfloat16)
        queries_to[t][0]()

    choose(2)
    choose(3)
    nb_copies[1].start()
    zbuf1[h] = pick[2 + core, z]

    zsent(0)
    zsend(2)

    v_v[...] = jnp.ones_like(v_v)
    lane = lax.broadcasted_iota(jnp.int32, (1, 4 * C), 1)
    lane_slot = lax.shift_right_logical(lane, 7)
    lane_n = lax.shift_right_logical(lane, 3) & 15
    lane_k = jnp.where(lane_slot == OPP, 2, jnp.where(lane_slot == LEFT, 3, jnp.where(lane_slot == RIGHT, 1, 0)))
    lane_row = (cpos * cstep + ((kpos + lane_k) & 3) * kstep) * ROWS + (lane & 7)
    col = lax.broadcasted_iota(jnp.int32, (2 * C, C), 1)

    def mask(t):
        user = 2 * h + t
        idv = jnp.zeros((1, 4 * C), jnp.int32)
        for n in range(NSEL):
            idv = jnp.where(lane_n == n, sel_ref[n, user], idv)
        return jnp.where(idv * BLK + lane_row < len_ref[user], 0.0, -1e30).astype(jnp.float32)

    def compact(t):
        user = 2 * h + t
        own = [lax.shift_right_logical(sel_ref[n, user], 4) for n in range(NSEL)]
        pltpu.make_async_copy(zbuf[t].at[pl.ds(0, 15)], zbuf[t].at[pl.ds(0, 15)], zr_sem.at[t]).wait()
        for n in range(0, NSEL, 2):
            pair = []
            for m in (n, n + 1):
                later = jnp.int32(0)
                for o in range(m + 1, NSEL):
                    later = later | (own[o] == own[m]).astype(jnp.int32)
                both = zbuf[t][own[m]]
                pair.append(jnp.where(later == 0, both[:ROWS], both[ROWS:]))
            gat[t, OWN, n * ROWS:(n + 2) * ROWS] = jnp.concatenate(pair, axis=0)

    def project(t, slots):
        for s in slots:
            kv = jnp.dot(gat[t, s], kvw[...], preferred_element_type=jnp.float32).astype(jnp.bfloat16)
            k_v[s * C:(s + 1) * C] = kv[:, :D]
            for hd in range(HEADS):
                v_v[s * C:(s + 1) * C, hd * 256:hd * 256 + HD] = kv[:, D + hd * HD:D + (hd + 1) * HD]

    out_copies = {}

    def send_out(t, *slots):
        for s in slots:
            send_one(t, s)

    def send_one(t, s):
        to = cdev({OPP: 2, LEFT: 3, RIGHT: 1}[s])
        for kind, (src, dst, ssem, rsem) in enumerate(
            ((osend, orecv, os_sem, or_sem), (ostat, rstat, ss_sem, sr_sem))
        ):
            cp = pltpu.make_async_remote_copy(
                src_ref=src.at[t, s], dst_ref=dst.at[t, s], send_sem=ssem.at[t, s], recv_sem=rsem.at[t, s],
                device_id=to, device_id_type=MESH,
            )
            cp.start()
            out_copies[t, s, kind] = cp

    def attend(t, bias, pair):
        stat = jnp.zeros((2 * C, C), jnp.float32)
        parts = []
        for hd in range(HEADS):
            q = qall[t, pair:pair + 2, :, hd * HD:(hd + 1) * HD].reshape(2 * C, HD)
            s = lax.dot_general(q, k_v[:, hd * HD:(hd + 1) * HD], NT, preferred_element_type=jnp.float32) * SCALE + bias
            m = jnp.max(s, axis=1, keepdims=True)
            p = jnp.exp2(s - m).astype(jnp.bfloat16)
            o = jnp.dot(p, v_v[:, hd * 256:(hd + 1) * 256], preferred_element_type=jnp.float32)
            l = o[:, HD:]
            parts.append((o[:, :HD] / l).astype(jnp.bfloat16))
            stat = jnp.where(col == hd, m, stat)
            stat = jnp.where(col == HEADS + hd, l, stat)
        part = jnp.concatenate(parts, axis=1)
        stat = stat.T[:8]
        for i in range(2):
            s = pair + i
            if s == OWN:
                orecv[t, OWN] = part[i * C:(i + 1) * C]
                rstat[t, OWN] = stat[:, i * C:(i + 1) * C]
            else:
                osend[t, s] = part[i * C:(i + 1) * C]
                ostat[t, s] = stat[:, i * C:(i + 1) * C]

    def finish(t):
        for s in (OPP, LEFT, RIGHT):
            for kind in range(2):
                out_copies[t, s, kind].wait_recv()
        stats = [rstat[t, k] for k in range(4)]
        top = jnp.maximum(jnp.maximum(stats[0][:4], stats[1][:4]), jnp.maximum(stats[2][:4], stats[3][:4]))
        parts = [s[4:] * jnp.exp2(s[:4] - top) for s in stats]
        total = (parts[0] + parts[1]) + (parts[2] + parts[3])
        wts = jnp.concatenate([p / total for p in parts] + [jnp.zeros((C - 16, C), jnp.float32)], axis=0).T
        mixed = []
        for hd in range(HEADS):
            acc = jnp.zeros((C, HD), jnp.float32)
            for k in range(4):
                acc = acc + wts[:, 4 * k + hd:4 * k + hd + 1] * orecv[t, k, :, hd * HD:(hd + 1) * HD].astype(jnp.float32)
            mixed.append(acc.astype(jnp.bfloat16))
        mixed = jnp.concatenate(mixed, axis=1)
        out_ref[t] = jnp.dot(mixed, ow[...], preferred_element_type=jnp.float32).astype(jnp.bfloat16)

    bias0, bias1 = mask(0), mask(1)
    zsent(1)
    zsend(3)
    compact(0)
    rows_to[0][0]()
    small[2].wait()
    project(0, (OWN,))
    rows_to[0][1](LEFT, RIGHT)
    project(0, (LEFT, RIGHT))
    compact(1)
    rows_to[1][0]()
    rows_to[0][1](OPP)
    project(0, (OPP,))
    queries_to[0][1](OPP, LEFT, RIGHT)
    attend(0, bias0, 0)
    attend(0, bias0, 2)
    rows_to[1][2]()
    send_out(0, OPP, LEFT, RIGHT)
    project(1, (OWN,))
    rows_to[1][1](LEFT, RIGHT)
    project(1, (LEFT, RIGHT))
    rows_to[1][1](OPP)
    project(1, (OPP,))
    queries_to[1][1](OPP, LEFT, RIGHT)
    attend(1, bias1, 0)
    send_out(1, OPP, LEFT)
    attend(1, bias1, 2)
    send_out(1, RIGHT)
    small[3].wait()
    finish(0)
    finish(1)

    rows_to[0][2]()
    for t in range(2):
        queries_to[t][2]()
        zsent(2 + t)
        nb_copies[t].wait_send()
    for cp in out_copies.values():
        cp.wait_send()


def per_device(history, candidates, selected, lengths, kv_weight, query_weight, out_weight):
    smem = pl.BlockSpec(memory_space=pltpu.SMEM)
    any_ = pl.BlockSpec(memory_space=pl.ANY)
    bf = jnp.bfloat16
    dma = pltpu.SemaphoreType.DMA
    return pl.pallas_call(
        kernel,
        out_shape=jax.ShapeDtypeStruct((2, C, D), bf),
        in_specs=[smem, smem, any_, any_, any_, any_, any_],
        out_specs=pl.BlockSpec(memory_space=pltpu.VMEM),
        scratch_shapes=[pltpu.VMEM((8, LB, ROWS, D), bf)] * 4
        + [pltpu.VMEM((4, 8, 2 * ROWS, D), bf)]
        + [pltpu.VMEM((OWN_RANGES, 2 * ROWS, D), bf)] * 2
        + [
            pltpu.VMEM((2, C, D), bf),
            pltpu.VMEM((D, 2 * D), bf),
            pltpu.VMEM((D, D), bf),
            pltpu.VMEM((D, D), bf),
            pltpu.VMEM((2, 4, C, D), bf),
            pltpu.VMEM((2, 4, C, D), bf),
            pltpu.VMEM((4 * C, D), bf),
            pltpu.VMEM((4 * C, HEADS * 256), bf),
            pltpu.VMEM((2, 3, C, D), bf),
            pltpu.VMEM((2, 3, 8, C), jnp.float32),
            pltpu.VMEM((2, 4, C, D), bf),
            pltpu.VMEM((2, 4, 8, C), jnp.float32),
            dma((8,)),
            dma((4,)), dma((2,)), dma((2,)),
            dma((2, 3)), dma((2, 3)),
            dma((2, 3)), dma((2, 3)),
            dma((2, 3)), dma((2, 3)),
            dma((2, 3)), dma((2, 3)),
        ],
        compiler_params=pltpu.CompilerParams(
            collective_id=0, has_side_effects=True, vmem_limit_bytes=60 * 1024 * 1024
        ),
    )(selected.T, lengths, history.reshape(8, 4, LB, ROWS, D), candidates, kv_weight, query_weight, out_weight)


def solution(mesh):
    return jax.shard_map(
        per_device,
        mesh=mesh,
        in_specs=(P(None, "hist", "cand", None), P("hist", "cand", None), P(), P(), P(), P(), P()),
        out_specs=P("hist", "cand", None),
        check_vma=False,
    )
```

```python
import jax
import jax.numpy as jnp
from jax import lax
from jax.experimental import pallas as pl
from jax.experimental.pallas import tpu as pltpu
from jax.sharding import PartitionSpec as P

MESH = pl.DeviceIdType.MESH
HEADS = 4
HD = 128
BLK = 128
NSEL = 16
D = 512
U = 32
LB = 16
OWN_RANGES = 16
ROWS = 8
C = 128
HALF = C // 2
SCALE = HD ** -0.5 * 1.4426950408889634
NT = (((1,), (1,)), ((), ()))
OPP, OWN, LEFT, RIGHT = 0, 1, 2, 3


def spread(buf, peers, send_sem, recv_sem):
    copies = {
        s: pltpu.make_async_remote_copy(
            src_ref=buf.at[OWN], dst_ref=buf.at[s], send_sem=send_sem.at[s], recv_sem=recv_sem.at[s],
            device_id=peers[s], device_id_type=MESH,
        )
        for s in (OPP, LEFT, RIGHT)
    }

    def start(*slots):
        for s in slots:
            copies[s].start()

    def arrived(*slots):
        for s in slots:
            copies[s].wait_recv()

    def sent():
        for cp in copies.values():
            cp.wait_send()

    return start, arrived, sent


def kernel(meta_hbm, hist_hbm, cand_hbm, kvw_hbm, qw_hbm, ow_hbm, out_ref,
           hist0, hist1, hist2, hist3, pick, zbuf0, zbuf1, cand_v, kvw, qw, ow, gat, qall, k_v, v_v,
           osend, ostat, orecv, rstat, sel_ref,
           in_sem, zs_sem, zr_sem, nb_sem, xs_sem, xr_sem, qs_sem, qr_sem, os_sem, or_sem, ss_sem, sr_sem):
    hist_v = (hist0, hist1, hist2, hist3)
    zbuf = (zbuf0, zbuf1)
    h = lax.axis_index("hist")
    c = lax.axis_index("cand")
    z, core = h // 2, h % 2
    y, x = c // 4, c % 4
    sibling = (2 * z + 1 - core, c)

    kpos = jnp.where(core == 0, x, y)
    cpos = jnp.where(core == 0, y, x)
    kstep = jnp.where(core == 0, 1, 4)
    cstep = 5 - kstep

    def kdev(d):
        return (h, cpos * cstep + ((kpos + d) & 3) * kstep)

    def cdev(d):
        return (h, ((cpos + d) & 3) * cstep + kpos * kstep)

    kpeers = {OPP: kdev(2), LEFT: kdev(1), RIGHT: kdev(3)}
    cpeers = {OPP: cdev(2), LEFT: cdev(1), RIGHT: cdev(3)}

    hist_copies = [
        pltpu.make_async_copy(hist_hbm.at[:, 2 * (p % 2) + p // 2], hist_v[p], in_sem.at[p]) for p in range(4)
    ]
    small = [
        pltpu.make_async_copy(cand_hbm, cand_v, in_sem.at[4]),
        pltpu.make_async_copy(qw_hbm, qw, in_sem.at[5]),
        pltpu.make_async_copy(kvw_hbm, kvw, in_sem.at[6]),
        pltpu.make_async_copy(ow_hbm, ow, in_sem.at[7]),
    ]
    ids = pltpu.make_async_copy(meta_hbm, sel_ref, in_sem.at[8])
    for cp in [ids] + hist_copies:
        cp.start()

    zorder = (4, 3, 5, 2, 6, 1, 7)
    zpeers = [lax.rem(z + dz, 8) for dz in zorder]

    barrier = pltpu.get_barrier_semaphore()
    for zp in zpeers:
        for k in range(2):
            pl.semaphore_signal(barrier, inc=1, device_id=(2 * zp + k, c), device_id_type=MESH)
    for dev in [sibling] + [f(d) for f in (kdev, cdev) for d in (2, 1, 3)]:
        pl.semaphore_signal(barrier, inc=1, device_id=dev, device_id_type=MESH)

    for cp in small:
        cp.start()
    ids.wait()

    def choose(p):
        hist_copies[p].wait()

        def one_user(zp, carry):
            u = 4 * zp + 2 * (p % 2) + p // 2
            first = jnp.int32(0)
            second = jnp.int32(0)
            for n in range(NSEL):
                one = sel_ref[n, u]
                mine = lax.shift_right_logical(one, 4) == h
                second = jnp.where(mine, first, second)
                first = jnp.where(mine, one & 15, first)
            pick[p, zp] = jnp.concatenate([hist_v[p][zp, first], hist_v[p][zp, second]], axis=0)
            return carry

        lax.fori_loop(0, 8, one_user, 0)

    def zsend(p):
        for zp in zpeers:
            pltpu.make_async_remote_copy(
                src_ref=pick.at[p, zp], dst_ref=zbuf[p // 2].at[h], send_sem=zs_sem.at[p], recv_sem=zr_sem.at[p // 2],
                device_id=(2 * zp + p % 2, c), device_id_type=MESH,
            ).start()

    def zsent(p):
        pltpu.make_async_copy(zbuf0.at[pl.ds(0, 7)], zbuf0.at[pl.ds(0, 7)], zs_sem.at[p]).wait()

    nb_copies = [
        pltpu.make_async_remote_copy(
            src_ref=pick.at[2 * t + 1 - core, z], dst_ref=zbuf[t].at[h], send_sem=nb_sem.at[t], recv_sem=zr_sem.at[t],
            device_id=sibling, device_id_type=MESH,
        )
        for t in range(2)
    ]

    choose(0)
    pl.semaphore_wait(barrier, 21)
    zsend(0)
    choose(1)
    zsend(1)
    nb_copies[0].start()
    zbuf0[h] = pick[core, z]

    small[0].wait()
    small[1].wait()
    rows_to = [spread(gat.at[t], kpeers, xs_sem.at[t], xr_sem.at[t]) for t in range(2)]
    queries_to = [spread(qall.at[t], cpeers, qs_sem.at[t], qr_sem.at[t]) for t in range(2)]
    for t in range(2):
        qall[t, OWN] = jnp.dot(cand_v[t], qw[...], preferred_element_type=jnp.float32).astype(jnp.bfloat16)
        queries_to[t][0](OPP, LEFT, RIGHT)

    choose(2)
    choose(3)
    nb_copies[1].start()
    zbuf1[h] = pick[2 + core, z]

    zsent(0)
    zsend(2)

    v_v[...] = jnp.ones_like(v_v)
    lane = lax.broadcasted_iota(jnp.int32, (1, 4 * C), 1)
    lane_slot = lax.shift_right_logical(lane, 7)
    lane_n = lax.shift_right_logical(lane, 3) & 15
    lane_k = jnp.where(lane_slot == OPP, 2, jnp.where(lane_slot == LEFT, 3, jnp.where(lane_slot == RIGHT, 1, 0)))
    lane_row = (cpos * cstep + ((kpos + lane_k) & 3) * kstep) * ROWS + (lane & 7)
    col = lax.broadcasted_iota(jnp.int32, (2 * C, C), 1)

    def mask(t):
        user = 2 * h + t
        idv = jnp.zeros((1, 4 * C), jnp.int32)
        for n in range(NSEL):
            idv = jnp.where(lane_n == n, sel_ref[n, user], idv)
        return jnp.where(idv * BLK + lane_row < sel_ref[NSEL, user], 0.0, -1e30).astype(jnp.float32)

    def places(t):
        own = [lax.shift_right_logical(sel_ref[n, 2 * h + t], 4) for n in range(NSEL)]
        second = []
        for n in range(NSEL):
            later = jnp.int32(0)
            for o in range(n + 1, NSEL):
                later = later | (own[o] == own[n]).astype(jnp.int32)
            second.append(later)
        return own, second

    def compact(t, own, second):
        pltpu.make_async_copy(zbuf[t].at[pl.ds(0, 15)], zbuf[t].at[pl.ds(0, 15)], zr_sem.at[t]).wait()
        for n in range(0, NSEL, 2):
            pair = []
            for m in (n, n + 1):
                both = zbuf[t][own[m]]
                pair.append(jnp.where(second[m] == 0, both[:ROWS], both[ROWS:]))
            gat[t, OWN, n * ROWS:(n + 2) * ROWS] = jnp.concatenate(pair, axis=0)

    def project(t, slots):
        for s in slots:
            kv = jnp.dot(gat[t, s], kvw[...], preferred_element_type=jnp.float32).astype(jnp.bfloat16)
            k_v[s * C:(s + 1) * C] = kv[:, :D]
            for hd in range(HEADS):
                v_v[s * C:(s + 1) * C, hd * 256:hd * 256 + HD] = kv[:, D + hd * HD:D + (hd + 1) * HD]

    out_copies = {}

    def send_out(t, *slots):
        for s in slots:
            send_one(t, s)

    def send_one(t, s):
        to = cdev({OPP: 2, LEFT: 3, RIGHT: 1}[s])
        for kind, (src, dst, ssem, rsem) in enumerate(
            ((osend, orecv, os_sem, or_sem), (ostat, rstat, ss_sem, sr_sem))
        ):
            cp = pltpu.make_async_remote_copy(
                src_ref=src.at[t, s], dst_ref=dst.at[t, s], send_sem=ssem.at[t, s], recv_sem=rsem.at[t, s],
                device_id=to, device_id_type=MESH,
            )
            cp.start()
            out_copies[t, s, kind] = cp

    def attend(t, bias, pair):
        stat = jnp.zeros((2 * C, C), jnp.float32)
        parts = []
        for hd in range(HEADS):
            q = qall[t, pair:pair + 2, :, hd * HD:(hd + 1) * HD].reshape(2 * C, HD)
            s = lax.dot_general(q, k_v[:, hd * HD:(hd + 1) * HD], NT, preferred_element_type=jnp.float32) * SCALE + bias
            m = jnp.max(s, axis=1, keepdims=True)
            p = jnp.exp2(s - m).astype(jnp.bfloat16)
            o = jnp.dot(p, v_v[:, hd * 256:(hd + 1) * 256], preferred_element_type=jnp.float32)
            parts.append(o[:, :HD].astype(jnp.bfloat16))
            stat = jnp.where(col == hd, m, stat)
            stat = jnp.where(col == HEADS + hd, o[:, HD:], stat)
        part = jnp.concatenate(parts, axis=1)
        stat = stat.T[:8]
        for i in range(2):
            s = pair + i
            if s == OWN:
                orecv[t, OWN] = part[i * C:(i + 1) * C]
                rstat[t, OWN] = stat[:, i * C:(i + 1) * C]
            else:
                osend[t, s] = part[i * C:(i + 1) * C]
                ostat[t, s] = stat[:, i * C:(i + 1) * C]

    def finish(t):
        for s in (OPP, LEFT, RIGHT):
            for kind in range(2):
                out_copies[t, s, kind].wait_recv()
        stats = [rstat[t, k] for k in range(4)]
        top = jnp.maximum(jnp.maximum(stats[0][:4], stats[1][:4]), jnp.maximum(stats[2][:4], stats[3][:4]))
        parts = [jnp.exp2(s[:4] - top) for s in stats]
        sums = [p * s[4:] for p, s in zip(parts, stats)]
        total = (sums[0] + sums[1]) + (sums[2] + sums[3])
        wts = jnp.concatenate([p / total for p in parts] + [jnp.zeros((C - 16, C), jnp.float32)], axis=0).T
        mixed = []
        for hd in range(HEADS):
            acc = jnp.zeros((C, HD), jnp.float32)
            for k in range(4):
                acc = acc + wts[:, 4 * k + hd:4 * k + hd + 1] * orecv[t, k, :, hd * HD:(hd + 1) * HD].astype(jnp.float32)
            mixed.append(acc.astype(jnp.bfloat16))
        mixed = jnp.concatenate(mixed, axis=1)
        out_ref[t] = jnp.dot(mixed, ow[...], preferred_element_type=jnp.float32).astype(jnp.bfloat16)

    bias0, bias1 = mask(0), mask(1)
    places0, places1 = places(0), places(1)
    zsent(1)
    zsend(3)
    compact(0, *places0)
    rows_to[0][0](OPP, LEFT, RIGHT)
    small[2].wait()
    project(0, (OWN,))
    compact(1, *places1)
    rows_to[1][0](OPP, LEFT, RIGHT)
    rows_to[0][1](LEFT, RIGHT)
    project(0, (LEFT, RIGHT))
    rows_to[0][1](OPP)
    project(0, (OPP,))
    queries_to[0][1](OPP, LEFT, RIGHT)
    attend(0, bias0, 0)
    attend(0, bias0, 2)
    rows_to[1][2]()
    send_out(0, OPP, LEFT, RIGHT)
    project(1, (OWN,))
    rows_to[1][1](LEFT, RIGHT)
    project(1, (LEFT, RIGHT))
    rows_to[1][1](OPP)
    project(1, (OPP,))
    queries_to[1][1](OPP, LEFT, RIGHT)
    attend(1, bias1, 0)
    send_out(1, OPP)
    attend(1, bias1, 2)
    send_out(1, LEFT, RIGHT)
    small[3].wait()
    finish(0)
    finish(1)

    rows_to[0][2]()
    for t in range(2):
        queries_to[t][2]()
        zsent(2 + t)
        nb_copies[t].wait_send()
    for cp in out_copies.values():
        cp.wait_send()


def per_device(history, candidates, selected, lengths, kv_weight, query_weight, out_weight):
    any_ = pl.BlockSpec(memory_space=pl.ANY)
    bf = jnp.bfloat16
    dma = pltpu.SemaphoreType.DMA
    return pl.pallas_call(
        kernel,
        out_shape=jax.ShapeDtypeStruct((2, C, D), bf),
        in_specs=[any_] * 6,
        out_specs=pl.BlockSpec(memory_space=pltpu.VMEM),
        scratch_shapes=[pltpu.VMEM((8, LB, ROWS, D), bf)] * 4
        + [pltpu.VMEM((4, 8, 2 * ROWS, D), bf)]
        + [pltpu.VMEM((OWN_RANGES, 2 * ROWS, D), bf)] * 2
        + [
            pltpu.VMEM((2, C, D), bf),
            pltpu.VMEM((D, 2 * D), bf),
            pltpu.VMEM((D, D), bf),
            pltpu.VMEM((D, D), bf),
            pltpu.VMEM((2, 4, C, D), bf),
            pltpu.VMEM((2, 4, C, D), bf),
            pltpu.VMEM((4 * C, D), bf),
            pltpu.VMEM((4 * C, HEADS * 256), bf),
            pltpu.VMEM((2, 4, C, D), bf),
            pltpu.VMEM((2, 4, 8, C), jnp.float32),
            pltpu.VMEM((2, 4, C, D), bf),
            pltpu.VMEM((2, 4, 8, C), jnp.float32),
            pltpu.SMEM((NSEL + 1, U), jnp.int32),
            dma((9,)),
            dma((4,)), dma((2,)), dma((2,)),
            dma((2, 4)), dma((2, 4)),
            dma((2, 4)), dma((2, 4)),
            dma((2, 4)), dma((2, 4)),
            dma((2, 4)), dma((2, 4)),
        ],
        compiler_params=pltpu.CompilerParams(
            collective_id=0, has_side_effects=True, vmem_limit_bytes=56098816
        ),
    )(jnp.concatenate([selected.T, lengths[None]], axis=0), history.reshape(8, 4, LB, ROWS, D), candidates, kv_weight, query_weight, out_weight)


def solution(mesh):
    return jax.shard_map(
        per_device,
        mesh=mesh,
        in_specs=(P(None, "hist", "cand", None), P("hist", "cand", None), P(), P(), P(), P(), P()),
        out_specs=P("hist", "cand", None),
        check_vma=False,
    )
```

```python
import jax
import jax.numpy as jnp
from jax import lax
from jax.experimental import pallas as pl
from jax.experimental.pallas import tpu as pltpu
from jax.sharding import PartitionSpec as P

MESH = pl.DeviceIdType.MESH
HEADS = 4
HD = 128
BLK = 128
NSEL = 16
D = 512
U = 32
LB = 16
OWN_RANGES = 16
ROWS = 8
C = 128
HALF = C // 2
SCALE = HD ** -0.5 * 1.4426950408889634
NT = (((1,), (1,)), ((), ()))
OPP, LEFT, RIGHT, OWN = 0, 1, 2, 3
OFFSET = {OPP: 2, LEFT: 3, RIGHT: 1}


def spread(buf, peers, send_sem, recv_sem):
    copies = [
        pltpu.make_async_remote_copy(
            src_ref=buf.at[OWN], dst_ref=buf.at[s], send_sem=send_sem.at[s], recv_sem=recv_sem.at[s],
            device_id=peers[s], device_id_type=MESH,
        )
        for s in (OPP, LEFT, RIGHT)
    ]

    def start():
        for cp in copies:
            cp.start()

    def arrived(*slots):
        for s in slots:
            copies[s].wait_recv()

    def sent():
        for cp in copies:
            cp.wait_send()

    return start, arrived, sent


def kernel(meta_hbm, hist_hbm, cand_hbm, kvw_hbm, qw_hbm, ow_hbm, out_ref,
           hist0, hist1, hist2, hist3, pick, zbuf0, zbuf1, cand_v, kvw, qw, ow, gat, qall, k_v, v_v,
           osend, ostat, orecv, rstat, sel_ref,
           in_sem, zs_sem, zr_sem, nb_sem, xs_sem, xr_sem, qs_sem, qr_sem, os_sem, or_sem, ss_sem, sr_sem):
    hist_v = (hist0, hist1, hist2, hist3)
    zbuf = (zbuf0, zbuf1)
    h = lax.axis_index("hist")
    c = lax.axis_index("cand")
    z, core = h // 2, h % 2
    y, x = c // 4, c % 4
    sibling = (2 * z + 1 - core, c)

    kpos = jnp.where(core == 0, x, y)
    cpos = jnp.where(core == 0, y, x)
    kstep = jnp.where(core == 0, 1, 4)
    cstep = 5 - kstep

    def kdev(d):
        return (h, cpos * cstep + ((kpos + d) & 3) * kstep)

    def cdev(d):
        return (h, ((cpos + d) & 3) * cstep + kpos * kstep)

    kpeers = {OPP: kdev(2), LEFT: kdev(1), RIGHT: kdev(3)}
    cpeers = {OPP: cdev(2), LEFT: cdev(1), RIGHT: cdev(3)}

    hist_copies = [
        pltpu.make_async_copy(hist_hbm.at[:, 2 * (p % 2) + p // 2], hist_v[p], in_sem.at[p]) for p in range(4)
    ]
    small = [
        pltpu.make_async_copy(cand_hbm, cand_v, in_sem.at[4]),
        pltpu.make_async_copy(qw_hbm, qw, in_sem.at[5]),
        pltpu.make_async_copy(kvw_hbm, kvw, in_sem.at[6]),
        pltpu.make_async_copy(ow_hbm, ow, in_sem.at[7]),
    ]
    ids = pltpu.make_async_copy(meta_hbm, sel_ref, in_sem.at[8])
    for cp in [ids] + hist_copies:
        cp.start()

    zorder = (4, 3, 5, 2, 6, 1, 7)
    zpeers = [lax.rem(z + dz, 8) for dz in zorder]

    barrier = pltpu.get_barrier_semaphore()
    for zp in zpeers:
        for k in range(2):
            pl.semaphore_signal(barrier, inc=1, device_id=(2 * zp + k, c), device_id_type=MESH)
    for dev in [sibling] + [f(d) for f in (kdev, cdev) for d in (2, 1, 3)]:
        pl.semaphore_signal(barrier, inc=1, device_id=dev, device_id_type=MESH)

    for cp in small:
        cp.start()
    ids.wait()

    def choose(p):
        hist_copies[p].wait()

        def one_user(zp, carry):
            u = 4 * zp + 2 * (p % 2) + p // 2
            first = jnp.int32(0)
            second = jnp.int32(0)
            for n in range(NSEL):
                one = sel_ref[n, u]
                mine = lax.shift_right_logical(one, 4) == h
                second = jnp.where(mine, first, second)
                first = jnp.where(mine, one & 15, first)
            pick[p, zp] = jnp.concatenate([hist_v[p][zp, first], hist_v[p][zp, second]], axis=0)
            return carry

        lax.fori_loop(0, 8, one_user, 0)

    def zsend(p):
        for zp in zpeers:
            pltpu.make_async_remote_copy(
                src_ref=pick.at[p, zp], dst_ref=zbuf[p // 2].at[h], send_sem=zs_sem.at[p], recv_sem=zr_sem.at[p // 2],
                device_id=(2 * zp + p % 2, c), device_id_type=MESH,
            ).start()

    def zsent(p):
        pltpu.make_async_copy(zbuf0.at[pl.ds(0, 7)], zbuf0.at[pl.ds(0, 7)], zs_sem.at[p]).wait()

    nb_copies = [
        pltpu.make_async_remote_copy(
            src_ref=pick.at[2 * t + 1 - core, z], dst_ref=zbuf[t].at[h], send_sem=nb_sem.at[t], recv_sem=zr_sem.at[t],
            device_id=sibling, device_id_type=MESH,
        )
        for t in range(2)
    ]

    choose(0)
    pl.semaphore_wait(barrier, 21)
    zsend(0)
    choose(1)
    zsend(1)
    nb_copies[0].start()
    zbuf0[h] = pick[core, z]

    small[0].wait()
    small[1].wait()
    rows_to = [spread(gat.at[t], kpeers, xs_sem.at[t], xr_sem.at[t]) for t in range(2)]
    queries_to = [spread(qall.at[t], cpeers, qs_sem.at[t], qr_sem.at[t]) for t in range(2)]
    for t in range(2):
        qall[t, OWN] = jnp.dot(cand_v[t], qw[...], preferred_element_type=jnp.float32).astype(jnp.bfloat16)
        queries_to[t][0]()

    choose(2)
    choose(3)
    nb_copies[1].start()
    zbuf1[h] = pick[2 + core, z]

    zsent(0)
    zsend(2)

    v_v[...] = jnp.ones_like(v_v)
    lane = lax.broadcasted_iota(jnp.int32, (1, 4 * C), 1)
    lane_slot = lax.shift_right_logical(lane, 7)
    lane_n = lax.shift_right_logical(lane, 3) & 15
    lane_k = jnp.where(lane_slot == OPP, 2, jnp.where(lane_slot == LEFT, 3, jnp.where(lane_slot == RIGHT, 1, 0)))
    lane_row = (cpos * cstep + ((kpos + lane_k) & 3) * kstep) * ROWS + (lane & 7)
    col = lax.broadcasted_iota(jnp.int32, (4 * C, C), 1)

    def mask(t):
        user = 2 * h + t
        idv = jnp.zeros((1, 4 * C), jnp.int32)
        for n in range(NSEL):
            idv = jnp.where(lane_n == n, sel_ref[n, user], idv)
        return jnp.where(idv * BLK + lane_row < sel_ref[NSEL, user], 0.0, -1e30).astype(jnp.float32)

    def places(t):
        own = [lax.shift_right_logical(sel_ref[n, 2 * h + t], 4) for n in range(NSEL)]
        second = []
        for n in range(NSEL):
            later = jnp.int32(0)
            for o in range(n + 1, NSEL):
                later = later | (own[o] == own[n]).astype(jnp.int32)
            second.append(later)
        return own, second

    def compact(t, own, second):
        pltpu.make_async_copy(zbuf[t].at[pl.ds(0, 15)], zbuf[t].at[pl.ds(0, 15)], zr_sem.at[t]).wait()
        for n in range(0, NSEL, 2):
            pair = []
            for m in (n, n + 1):
                both = zbuf[t][own[m]]
                pair.append(jnp.where(second[m] == 0, both[:ROWS], both[ROWS:]))
            gat[t, OWN, n * ROWS:(n + 2) * ROWS] = jnp.concatenate(pair, axis=0)

    def project(t, slots):
        for s in slots:
            kv = jnp.dot(gat[t, s], kvw[...], preferred_element_type=jnp.float32).astype(jnp.bfloat16)
            k_v[s * C:(s + 1) * C] = kv[:, :D]
            for hd in range(HEADS):
                v_v[s * C:(s + 1) * C, hd * 256:hd * 256 + HD] = kv[:, D + hd * HD:D + (hd + 1) * HD]

    out_copies = [[], []]

    def send_out(t, heads):
        for s in (OPP, LEFT, RIGHT):
            cp = pltpu.make_async_remote_copy(
                src_ref=osend.at[t, s, heads], dst_ref=orecv.at[t, s, heads],
                send_sem=os_sem.at[t, s, heads.start], recv_sem=or_sem.at[t, s, heads.start],
                device_id=cdev(OFFSET[s]), device_id_type=MESH,
            )
            cp.start()
            out_copies[t].append(cp)

    def send_stat(t, heads):
        for s in (OPP, LEFT, RIGHT):
            cp = pltpu.make_async_remote_copy(
                src_ref=ostat.at[t, s, heads], dst_ref=rstat.at[t, s, heads],
                send_sem=ss_sem.at[t, s, heads.start], recv_sem=sr_sem.at[t, s, heads.start],
                device_id=cdev(OFFSET[s]), device_id_type=MESH,
            )
            cp.start()
            out_copies[t].append(cp)

    def attend(t, bias, after_head):
        for hd in range(HEADS):
            q = qall[t, :, :, hd * HD:(hd + 1) * HD].reshape(4 * C, HD)
            s = lax.dot_general(q, k_v[:, hd * HD:(hd + 1) * HD], NT, preferred_element_type=jnp.float32) * SCALE + bias
            m = jnp.max(s, axis=1, keepdims=True)
            p = jnp.exp2(s - m).astype(jnp.bfloat16)
            o = jnp.dot(p, v_v[:, hd * 256:(hd + 1) * 256], preferred_element_type=jnp.float32)
            part = o[:, :HD].astype(jnp.bfloat16)
            stat = jnp.where(col == 0, m, o[:, HD:]).T[:8]
            for i in range(4):
                dst = orecv if i == OWN else osend
                dst[t, i, hd] = part[i * C:(i + 1) * C]
                dst = rstat if i == OWN else ostat
                dst[t, i, hd] = stat[:, i * C:(i + 1) * C]
            after_head(hd)

    def finish(t, by_head):
        acc = jnp.zeros((C, D), jnp.float32)
        if not by_head:
            for cp in out_copies[t]:
                cp.wait_recv()
        for hd in range(HEADS):
            if by_head:
                for cp in out_copies[t][6 * hd:6 * hd + 6]:
                    cp.wait_recv()
            stats = [rstat[t, k, hd] for k in range(4)]
            top = jnp.maximum(jnp.maximum(stats[0][:1], stats[1][:1]), jnp.maximum(stats[2][:1], stats[3][:1]))
            parts = [jnp.exp2(s[:1] - top) for s in stats]
            sums = [p * s[1:2] for p, s in zip(parts, stats)]
            total = (sums[0] + sums[1]) + (sums[2] + sums[3])
            wts = jnp.concatenate([p / total for p in parts] + [jnp.zeros((C - 4, C), jnp.float32)], axis=0).T
            mixed = jnp.zeros((C, HD), jnp.float32)
            for k in range(4):
                mixed = mixed + wts[:, k:k + 1] * orecv[t, k, hd].astype(jnp.float32)
            acc = acc + jnp.dot(
                mixed.astype(jnp.bfloat16), ow[hd * HD:(hd + 1) * HD], preferred_element_type=jnp.float32
            )
        out_ref[t] = acc.astype(jnp.bfloat16)

    bias0, bias1 = mask(0), mask(1)
    places0, places1 = places(0), places(1)
    zsent(1)
    zsend(3)
    compact(0, *places0)
    rows_to[0][0]()
    small[2].wait()
    project(0, (OWN,))
    compact(1, *places1)
    rows_to[1][0]()
    rows_to[0][1](LEFT, RIGHT)
    project(0, (LEFT, RIGHT))
    rows_to[0][1](OPP)
    project(0, (OPP,))
    queries_to[0][1](OPP, LEFT, RIGHT)
    attend(0, bias0, lambda hd: None)
    rows_to[1][2]()
    send_out(0, pl.ds(0, HEADS))
    send_stat(0, pl.ds(0, HEADS))
    project(1, (OWN,))
    rows_to[1][1](LEFT, RIGHT)
    project(1, (LEFT, RIGHT))
    rows_to[1][1](OPP)
    project(1, (OPP,))
    queries_to[1][1](OPP, LEFT, RIGHT)

    def send_head(hd):
        send_stat(1, pl.ds(hd, 1))
        send_out(1, pl.ds(hd, 1))

    attend(1, bias1, send_head)
    small[3].wait()
    finish(0, False)
    finish(1, True)

    rows_to[0][2]()
    for t in range(2):
        queries_to[t][2]()
        zsent(2 + t)
        nb_copies[t].wait_send()
    for cp in out_copies[0] + out_copies[1]:
        cp.wait_send()


def per_device(history, candidates, selected, lengths, kv_weight, query_weight, out_weight):
    any_ = pl.BlockSpec(memory_space=pl.ANY)
    bf = jnp.bfloat16
    dma = pltpu.SemaphoreType.DMA
    return pl.pallas_call(
        kernel,
        out_shape=jax.ShapeDtypeStruct((2, C, D), bf),
        in_specs=[any_] * 6,
        out_specs=pl.BlockSpec(memory_space=pltpu.VMEM),
        scratch_shapes=[pltpu.VMEM((8, LB, ROWS, D), bf)] * 4
        + [pltpu.VMEM((4, 8, 2 * ROWS, D), bf)]
        + [pltpu.VMEM((OWN_RANGES, 2 * ROWS, D), bf)] * 2
        + [
            pltpu.VMEM((2, C, D), bf),
            pltpu.VMEM((D, 2 * D), bf),
            pltpu.VMEM((D, D), bf),
            pltpu.VMEM((D, D), bf),
            pltpu.VMEM((2, 4, C, D), bf),
            pltpu.VMEM((2, 4, C, D), bf),
            pltpu.VMEM((4 * C, D), bf),
            pltpu.VMEM((4 * C, HEADS * 256), bf),
            pltpu.VMEM((2, 3, HEADS, C, HD), bf),
            pltpu.VMEM((2, 3, HEADS, 8, C), jnp.float32),
            pltpu.VMEM((2, 4, HEADS, C, HD), bf),
            pltpu.VMEM((2, 4, HEADS, 8, C), jnp.float32),
            pltpu.SMEM((NSEL + 1, U), jnp.int32),
            dma((9,)),
            dma((4,)), dma((2,)), dma((2,)),
            dma((2, 3)), dma((2, 3)),
            dma((2, 3)), dma((2, 3)),
            dma((2, 3, HEADS)), dma((2, 3, HEADS)),
            dma((2, 3, HEADS)), dma((2, 3, HEADS)),
        ],
        compiler_params=pltpu.CompilerParams(
            collective_id=0, has_side_effects=True, vmem_limit_bytes=56098816
        ),
    )(jnp.concatenate([selected.T, lengths[None]], axis=0), history.reshape(8, 4, LB, ROWS, D), candidates, kv_weight, query_weight, out_weight)


def solution(mesh):
    return jax.shard_map(
        per_device,
        mesh=mesh,
        in_specs=(P(None, "hist", "cand", None), P("hist", "cand", None), P(), P(), P(), P(), P()),
        out_specs=P("hist", "cand", None),
        check_vma=False,
    )
```

```python
import jax
import jax.numpy as jnp
from jax import lax
from jax.experimental import pallas as pl
from jax.experimental.pallas import tpu as pltpu
from jax.sharding import PartitionSpec as P

MESH = pl.DeviceIdType.MESH
HEADS = 4
HD = 128
BLK = 128
NSEL = 16
D = 512
U = 32
LB = 16
OWN_RANGES = 16
ROWS = 8
C = 128
HALF = C // 2
SCALE = HD ** -0.5 * 1.4426950408889634
NT = (((1,), (1,)), ((), ()))
OPP, LEFT, RIGHT, OWN = 0, 1, 2, 3
OFFSET = {OPP: 2, LEFT: 3, RIGHT: 1}


def spread(buf, peers, send_sem, recv_sem):
    copies = [
        pltpu.make_async_remote_copy(
            src_ref=buf.at[OWN], dst_ref=buf.at[s], send_sem=send_sem.at[s], recv_sem=recv_sem.at[s],
            device_id=peers[s], device_id_type=MESH,
        )
        for s in (OPP, LEFT, RIGHT)
    ]

    def start():
        for cp in copies:
            cp.start()

    def arrived(*slots):
        for s in slots:
            copies[s].wait_recv()

    def sent():
        for cp in copies:
            cp.wait_send()

    return start, arrived, sent


def kernel(meta_hbm, hist_hbm, cand_hbm, kvw_hbm, qw_hbm, ow_hbm, out_ref,
           hist0, hist1, hist2, hist3, pick, zbuf0, zbuf1, cand_v, kvw, qw, ow, gat, qall, k_v, v_v,
           osend, ostat, orecv, rstat, sel_ref,
           in_sem, zs_sem, zr_sem, nb_sem, xs_sem, xr_sem, qs_sem, qr_sem, os_sem, or_sem, ss_sem, sr_sem):
    hist_v = (hist0, hist1, hist2, hist3)
    zbuf = (zbuf0, zbuf1)
    h = lax.axis_index("hist")
    c = lax.axis_index("cand")
    z, core = h // 2, h % 2
    y, x = c // 4, c % 4
    sibling = (2 * z + 1 - core, c)

    swap = [core, 1 - core]
    kpos = [jnp.where(w == 0, x, y) for w in swap]
    cpos = [jnp.where(w == 0, y, x) for w in swap]
    kstep = [jnp.where(w == 0, 1, 4) for w in swap]
    cstep = [5 - k for k in kstep]

    def kdev(t, d):
        return (h, cpos[t] * cstep[t] + ((kpos[t] + d) & 3) * kstep[t])

    def cdev(t, d):
        return (h, ((cpos[t] + d) & 3) * cstep[t] + kpos[t] * kstep[t])

    kpeers = [{OPP: kdev(t, 2), LEFT: kdev(t, 1), RIGHT: kdev(t, 3)} for t in range(2)]
    cpeers = [{OPP: cdev(t, 2), LEFT: cdev(t, 1), RIGHT: cdev(t, 3)} for t in range(2)]

    hist_copies = [
        pltpu.make_async_copy(hist_hbm.at[:, 2 * (p % 2) + p // 2], hist_v[p], in_sem.at[p]) for p in range(4)
    ]
    small = [
        pltpu.make_async_copy(cand_hbm, cand_v, in_sem.at[4]),
        pltpu.make_async_copy(qw_hbm, qw, in_sem.at[5]),
        pltpu.make_async_copy(kvw_hbm, kvw, in_sem.at[6]),
        pltpu.make_async_copy(ow_hbm, ow, in_sem.at[7]),
    ]
    ids = pltpu.make_async_copy(meta_hbm, sel_ref, in_sem.at[8])
    for cp in [ids] + hist_copies:
        cp.start()

    zorder = (4, 3, 5, 2, 6, 1, 7)
    zpeers = [lax.rem(z + dz, 8) for dz in zorder]

    barrier = pltpu.get_barrier_semaphore()
    for zp in zpeers:
        for k in range(2):
            pl.semaphore_signal(barrier, inc=1, device_id=(2 * zp + k, c), device_id_type=MESH)
    for dev in [sibling] + [f(0, d) for f in (kdev, cdev) for d in (2, 1, 3)]:
        pl.semaphore_signal(barrier, inc=1, device_id=dev, device_id_type=MESH)

    for cp in small:
        cp.start()
    ids.wait()

    def choose(p):
        hist_copies[p].wait()

        def one_user(zp, carry):
            u = 4 * zp + 2 * (p % 2) + p // 2
            first = jnp.int32(0)
            second = jnp.int32(0)
            for n in range(NSEL):
                one = sel_ref[n, u]
                mine = lax.shift_right_logical(one, 4) == h
                second = jnp.where(mine, first, second)
                first = jnp.where(mine, one & 15, first)
            pick[p, zp] = jnp.concatenate([hist_v[p][zp, first], hist_v[p][zp, second]], axis=0)
            return carry

        lax.fori_loop(0, 8, one_user, 0)

    def zsend(p):
        for zp in zpeers:
            pltpu.make_async_remote_copy(
                src_ref=pick.at[p, zp], dst_ref=zbuf[p // 2].at[h], send_sem=zs_sem.at[p], recv_sem=zr_sem.at[p // 2],
                device_id=(2 * zp + p % 2, c), device_id_type=MESH,
            ).start()

    def zsent(p):
        pltpu.make_async_copy(zbuf0.at[pl.ds(0, 7)], zbuf0.at[pl.ds(0, 7)], zs_sem.at[p]).wait()

    nb_copies = [
        pltpu.make_async_remote_copy(
            src_ref=pick.at[2 * t + 1 - core, z], dst_ref=zbuf[t].at[h], send_sem=nb_sem.at[t], recv_sem=zr_sem.at[t],
            device_id=sibling, device_id_type=MESH,
        )
        for t in range(2)
    ]

    choose(0)
    pl.semaphore_wait(barrier, 21)
    zsend(0)
    choose(1)
    zsend(1)
    nb_copies[0].start()
    zbuf0[h] = pick[core, z]

    small[0].wait()
    small[1].wait()
    rows_to = [spread(gat.at[t], kpeers[t], xs_sem.at[t], xr_sem.at[t]) for t in range(2)]
    queries_to = [spread(qall.at[t], cpeers[t], qs_sem.at[t], qr_sem.at[t]) for t in range(2)]
    for t in range(2):
        qall[t, OWN] = jnp.dot(cand_v[t], qw[...], preferred_element_type=jnp.float32).astype(jnp.bfloat16)
        queries_to[t][0]()

    choose(2)
    choose(3)
    nb_copies[1].start()
    zbuf1[h] = pick[2 + core, z]

    zsent(0)
    zsend(2)

    v_v[...] = jnp.ones_like(v_v)
    lane = lax.broadcasted_iota(jnp.int32, (1, 4 * C), 1)
    lane_slot = lax.shift_right_logical(lane, 7)
    lane_n = lax.shift_right_logical(lane, 3) & 15
    lane_k = jnp.where(lane_slot == OPP, 2, jnp.where(lane_slot == LEFT, 3, jnp.where(lane_slot == RIGHT, 1, 0)))
    lane_row = [
        (cpos[t] * cstep[t] + ((kpos[t] + lane_k) & 3) * kstep[t]) * ROWS + (lane & 7) for t in range(2)
    ]
    col = lax.broadcasted_iota(jnp.int32, (4 * C, C), 1)

    def mask(t):
        user = 2 * h + t
        idv = jnp.zeros((1, 4 * C), jnp.int32)
        for n in range(NSEL):
            idv = jnp.where(lane_n == n, sel_ref[n, user], idv)
        return jnp.where(idv * BLK + lane_row[t] < sel_ref[NSEL, user], 0.0, -1e30).astype(jnp.float32)

    def places(t):
        own = [lax.shift_right_logical(sel_ref[n, 2 * h + t], 4) for n in range(NSEL)]
        second = []
        for n in range(NSEL):
            later = jnp.int32(0)
            for o in range(n + 1, NSEL):
                later = later | (own[o] == own[n]).astype(jnp.int32)
            second.append(later)
        return own, second

    def compact(t, own, second):
        pltpu.make_async_copy(zbuf[t].at[pl.ds(0, 15)], zbuf[t].at[pl.ds(0, 15)], zr_sem.at[t]).wait()
        for n in range(0, NSEL, 2):
            pair = []
            for m in (n, n + 1):
                both = zbuf[t][own[m]]
                pair.append(jnp.where(second[m] == 0, both[:ROWS], both[ROWS:]))
            gat[t, OWN, n * ROWS:(n + 2) * ROWS] = jnp.concatenate(pair, axis=0)

    def project(t, slots):
        for s in slots:
            kv = jnp.dot(gat[t, s], kvw[...], preferred_element_type=jnp.float32).astype(jnp.bfloat16)
            k_v[s * C:(s + 1) * C] = kv[:, :D]
            for hd in range(HEADS):
                v_v[s * C:(s + 1) * C, hd * 256:hd * 256 + HD] = kv[:, D + hd * HD:D + (hd + 1) * HD]

    out_copies = [[], []]

    def send_out(t, heads):
        for s in (OPP, LEFT, RIGHT):
            cp = pltpu.make_async_remote_copy(
                src_ref=osend.at[t, s, heads], dst_ref=orecv.at[t, s, heads],
                send_sem=os_sem.at[t, s, heads.start], recv_sem=or_sem.at[t, s, heads.start],
                device_id=cdev(t, OFFSET[s]), device_id_type=MESH,
            )
            cp.start()
            out_copies[t].append(cp)

    def send_stat(t, heads):
        for s in (OPP, LEFT, RIGHT):
            cp = pltpu.make_async_remote_copy(
                src_ref=ostat.at[t, s, heads], dst_ref=rstat.at[t, s, heads],
                send_sem=ss_sem.at[t, s, heads.start], recv_sem=sr_sem.at[t, s, heads.start],
                device_id=cdev(t, OFFSET[s]), device_id_type=MESH,
            )
            cp.start()
            out_copies[t].append(cp)

    def attend(t, bias, after_head):
        for hd in range(HEADS):
            q = qall[t, :, :, hd * HD:(hd + 1) * HD].reshape(4 * C, HD)
            s = lax.dot_general(q, k_v[:, hd * HD:(hd + 1) * HD], NT, preferred_element_type=jnp.float32) * SCALE + bias
            m = jnp.max(s, axis=1, keepdims=True)
            p = jnp.exp2(s - m).astype(jnp.bfloat16)
            o = jnp.dot(p, v_v[:, hd * 256:(hd + 1) * 256], preferred_element_type=jnp.float32)
            part = o[:, :HD].astype(jnp.bfloat16)
            stat = jnp.where(col == 0, m, o[:, HD:]).T[:8]
            for i in range(4):
                dst = orecv if i == OWN else osend
                dst[t, i, hd] = part[i * C:(i + 1) * C]
                dst = rstat if i == OWN else ostat
                dst[t, i, hd] = stat[:, i * C:(i + 1) * C]
            after_head(hd)

    def finish(t, by_head):
        acc = jnp.zeros((C, D), jnp.float32)
        if not by_head:
            for cp in out_copies[t]:
                cp.wait_recv()
        for hd in range(HEADS):
            if by_head:
                for cp in out_copies[t][6 * hd:6 * hd + 6]:
                    cp.wait_recv()
            stats = [rstat[t, k, hd] for k in range(4)]
            top = jnp.maximum(jnp.maximum(stats[0][:1], stats[1][:1]), jnp.maximum(stats[2][:1], stats[3][:1]))
            parts = [jnp.exp2(s[:1] - top) for s in stats]
            sums = [p * s[1:2] for p, s in zip(parts, stats)]
            total = (sums[0] + sums[1]) + (sums[2] + sums[3])
            wts = jnp.concatenate([p / total for p in parts] + [jnp.zeros((C - 4, C), jnp.float32)], axis=0).T
            mixed = jnp.zeros((C, HD), jnp.float32)
            for k in range(4):
                mixed = mixed + wts[:, k:k + 1] * orecv[t, k, hd].astype(jnp.float32)
            acc = acc + jnp.dot(
                mixed.astype(jnp.bfloat16), ow[hd * HD:(hd + 1) * HD], preferred_element_type=jnp.float32
            )
        out_ref[t] = acc.astype(jnp.bfloat16)

    bias0, bias1 = mask(0), mask(1)
    places0, places1 = places(0), places(1)
    zsent(1)
    zsend(3)
    compact(0, *places0)
    rows_to[0][0]()
    small[2].wait()
    project(0, (OWN,))
    compact(1, *places1)
    rows_to[1][0]()
    rows_to[0][1](LEFT, RIGHT)
    project(0, (LEFT, RIGHT))
    rows_to[0][1](OPP)
    project(0, (OPP,))
    queries_to[0][1](OPP, LEFT, RIGHT)
    attend(0, bias0, lambda hd: None)
    send_out(0, pl.ds(0, HEADS))
    send_stat(0, pl.ds(0, HEADS))
    project(1, (OWN,))
    rows_to[1][1](LEFT, RIGHT)
    project(1, (LEFT, RIGHT))
    rows_to[1][1](OPP)
    project(1, (OPP,))
    queries_to[1][1](OPP, LEFT, RIGHT)

    def send_head(hd):
        send_stat(1, pl.ds(hd, 1))
        send_out(1, pl.ds(hd, 1))

    attend(1, bias1, send_head)
    small[3].wait()
    finish(0, False)
    finish(1, True)

    rows_to[0][2]()
    rows_to[1][2]()
    for t in range(2):
        queries_to[t][2]()
        zsent(2 + t)
        nb_copies[t].wait_send()
    for cp in out_copies[0] + out_copies[1]:
        cp.wait_send()


def per_device(history, candidates, selected, lengths, kv_weight, query_weight, out_weight):
    any_ = pl.BlockSpec(memory_space=pl.ANY)
    bf = jnp.bfloat16
    dma = pltpu.SemaphoreType.DMA
    return pl.pallas_call(
        kernel,
        out_shape=jax.ShapeDtypeStruct((2, C, D), bf),
        in_specs=[any_] * 6,
        out_specs=pl.BlockSpec(memory_space=pltpu.VMEM),
        scratch_shapes=[pltpu.VMEM((8, LB, ROWS, D), bf)] * 4
        + [pltpu.VMEM((4, 8, 2 * ROWS, D), bf)]
        + [pltpu.VMEM((OWN_RANGES, 2 * ROWS, D), bf)] * 2
        + [
            pltpu.VMEM((2, C, D), bf),
            pltpu.VMEM((D, 2 * D), bf),
            pltpu.VMEM((D, D), bf),
            pltpu.VMEM((D, D), bf),
            pltpu.VMEM((2, 4, C, D), bf),
            pltpu.VMEM((2, 4, C, D), bf),
            pltpu.VMEM((4 * C, D), bf),
            pltpu.VMEM((4 * C, HEADS * 256), bf),
            pltpu.VMEM((2, 3, HEADS, C, HD), bf),
            pltpu.VMEM((2, 3, HEADS, 8, C), jnp.float32),
            pltpu.VMEM((2, 4, HEADS, C, HD), bf),
            pltpu.VMEM((2, 4, HEADS, 8, C), jnp.float32),
            pltpu.SMEM((NSEL + 1, U), jnp.int32),
            dma((9,)),
            dma((4,)), dma((2,)), dma((2,)),
            dma((2, 3)), dma((2, 3)),
            dma((2, 3)), dma((2, 3)),
            dma((2, 3, HEADS)), dma((2, 3, HEADS)),
            dma((2, 3, HEADS)), dma((2, 3, HEADS)),
        ],
        compiler_params=pltpu.CompilerParams(
            collective_id=0, has_side_effects=True, vmem_limit_bytes=56098816
        ),
    )(jnp.concatenate([selected.T, lengths[None]], axis=0), history.reshape(8, 4, LB, ROWS, D), candidates, kv_weight, query_weight, out_weight)


def solution(mesh):
    return jax.shard_map(
        per_device,
        mesh=mesh,
        in_specs=(P(None, "hist", "cand", None), P("hist", "cand", None), P(), P(), P(), P(), P()),
        out_specs=P("hist", "cand", None),
        check_vma=False,
    )
```
